128 devices in a mesh: gx: 32 (over z, y, x_hi), gy: 4 (over x_lo, core).
Axes of the slice: x: 4 (x_hi: 2, x_lo: 2; x = x_hi * 2 + x_lo), y: 4, z: 4, core: 2. Of those that a mesh axis runs over, the one named last changes fastest.
Arguments:
- tokens: bfloat16 [2048, 16384], P('gx', 'gy'), may hold values from -6 to 6
- gate_q: bfloat16 [16384, 28672], P('gy', 'gx'), may hold values from -4 to 4
- gate_scale: float32 [128, 224], P('gy', 'gx'), may hold values from 0.00234375 to 0.0234375
- up_q: bfloat16 [16384, 28672], P('gy', 'gx'), may hold values from -4 to 4
- up_scale: float32 [128, 224], P('gy', 'gx'), may hold values from 0.00234375 to 0.0234375
- down_q: bfloat16 [28672, 16384], P('gx', 'gy'), may hold values from -4 to 4
- down_scale: float32 [224, 128], P('gx', 'gy'), may hold values from 0.001775148 to 0.01775148
Outputs:
- mixed: bfloat16 [2048, 16384], P('gx', 'gy')
The draws below stay inside these ranges and needn't reach their ends.
All inputs are finite; a program needn't handle non-finite values.
Results may differ from the reference program's by a relative error of at most 0.035.
Values may be sent and summed in bfloat16 or wider, within the bound.
No kernel may reach another device: no remote copies, remote signals or barrier semaphores. Data moves between devices by JAX's collectives and lax.ppermute only.
A program may use at most 192 MiB of HBM per device.

```python
import math
import jax
import jax.numpy as jnp
from jax import lax

D = 16384
FF = 28672
TILE = 128
TOKENS = 2048
N_GX = 32
N_GY = 4


def shard_levels(stream_key, extent, pieces, low, top_value):
    gain = 1.0
    for axis_at, parts in pieces:
        steps = jax.random.uniform(jax.random.fold_in(jax.random.fold_in(stream_key, 6), axis_at), (parts,), jnp.float32, low / len(pieces), top_value / len(pieces))
        gain = gain * jnp.repeat(jnp.exp(steps), extent[axis_at] // parts).reshape((-1,) + (1,) * (len(extent) - 1 - axis_at))
    return gain


def gaussian(stream_key, dims, deviation, reach, shards=(), kind=jnp.bfloat16):
    entries = deviation * jax.random.normal(stream_key, dims, jnp.float32)
    if shards:
        entries = entries * shard_levels(stream_key, dims, shards, -0.22, 0.18)
    return jnp.clip(entries, -reach, reach).astype(kind)


def setup_inputs(seed: int = 0) -> dict:
    seeds = jax.random.split(jax.random.key(seed), 8)
    tokens = gaussian(seeds[0], (TOKENS, D), 1.0, 6.0, ((0, 32), (1, 4)))
    gate_q = gaussian(seeds[1], (D, FF), 1.0, 4.0, ((0, 4), (1, 32)))
    gate_scale = jnp.clip(jnp.exp(math.log(0.0234375) - 2.3025851 * jax.random.uniform(seeds[2], (D // TILE, FF // TILE), jnp.float32) ** shard_levels(seeds[2], (D // TILE, FF // TILE), ((0, 4), (1, 32)), -0.2, 0.2)), 0.00234375, 0.0234375)
    up_q = gaussian(seeds[3], (D, FF), 1.0, 4.0, ((0, 4), (1, 32)))
    up_scale = jnp.clip(jnp.exp(math.log(0.0234375) - 2.3025851 * jax.random.uniform(seeds[4], (D // TILE, FF // TILE), jnp.float32) ** shard_levels(seeds[4], (D // TILE, FF // TILE), ((0, 4), (1, 32)), -0.2, 0.2)), 0.00234375, 0.0234375)
    down_q = gaussian(seeds[5], (FF, D), 1.0, 4.0, ((0, 32), (1, 4)))
    down_scale = jnp.clip(jnp.exp(math.log(0.01775148) - 2.3025851 * jax.random.uniform(seeds[6], (FF // TILE, D // TILE), jnp.float32) ** shard_levels(seeds[6], (FF // TILE, D // TILE), ((0, 32), (1, 4)), -0.2, 0.2)), 0.001775148, 0.01775148)
    return {"tokens": tokens, "gate_q": gate_q, "gate_scale": gate_scale, "up_q": up_q, "up_scale": up_scale, "down_q": down_q, "down_scale": down_scale}


def dequant(values, scales):
    rows, cols = values.shape
    tiles = values.astype(jnp.float32).reshape(rows // 128, 128, cols // 128, 128) * scales[:, None, :, None]
    return tiles.reshape(rows, cols).astype(jnp.bfloat16)


def reference(tokens, gate_q, gate_scale, up_q, up_scale, down_q, down_scale):
    width = FF // N_GX
    group = D // N_GY

    def step(total, index):
        start = (index * width).astype(jnp.int32)
        tstart = (index * (width // 128)).astype(jnp.int32)
        gate_w = dequant(lax.dynamic_slice_in_dim(gate_q, start, width, 1), lax.dynamic_slice_in_dim(gate_scale, tstart, width // 128, 1))
        up_w = dequant(lax.dynamic_slice_in_dim(up_q, start, width, 1), lax.dynamic_slice_in_dim(up_scale, tstart, width // 128, 1))
        down_w = dequant(lax.dynamic_slice_in_dim(down_q, start, width, 0), lax.dynamic_slice_in_dim(down_scale, tstart, width // 128, 0))
        gate = jnp.zeros((TOKENS, width), jnp.float32)
        up = jnp.zeros((TOKENS, width), jnp.float32)
        for part in range(N_GY):
            lo = part * group
            feats = tokens[:, lo:lo + group]
            gate_part = jnp.dot(feats, gate_w[lo:lo + group], preferred_element_type=jnp.float32).astype(jnp.bfloat16)
            up_part = jnp.dot(feats, up_w[lo:lo + group], preferred_element_type=jnp.float32).astype(jnp.bfloat16)
            gate = gate + gate_part.astype(jnp.float32)
            up = up + up_part.astype(jnp.float32)
        hidden = (jax.nn.silu(gate) * up).astype(jnp.bfloat16)
        down_part = jnp.dot(hidden, down_w, preferred_element_type=jnp.float32).astype(jnp.bfloat16)
        return total + down_part.astype(jnp.float32), None

    total, _ = lax.scan(step, jnp.zeros((TOKENS, D), jnp.float32), jnp.arange(N_GX, dtype=jnp.int32))
    return total.astype(jnp.bfloat16)
```

```python
import jax
import jax.numpy as jnp
from jax import lax
from jax.experimental import pallas as pl
from jax.experimental.pallas import tpu as pltpu
from jax.sharding import Mesh
from jax.sharding import PartitionSpec as P

AXES = ("z", "y", "xh", "xl", "c")
SIZES = (4, 4, 2, 2, 2)
CHUNKS = 2


def index_of(z, y, xh, xl, c):
    return (((z * 4 + y) * 2 + xh) * 2 + xl) * 2 + c


def every_device():
    for z in range(4):
        for y in range(4):
            for xh in range(2):
                for xl in range(2):
                    for c in range(2):
                        yield z, y, xh, xl, c


def ring_pairs(outer, step):
    pairs = []
    for z, y, xh, xl, c in every_device():
        if (c == 0) == outer:
            there = ((z + step) % 4, y, xh, xl, c)
        else:
            there = (z, (y + step) % 4, xh, xl, c)
        pairs.append((index_of(z, y, xh, xl, c), index_of(*there)))
    return pairs


def ring(x, outer, step):
    return lax.ppermute(x, AXES, ring_pairs(outer, step))


def swap(x, axis):
    return lax.ppermute(x, axis, [(0, 1), (1, 0)])


def after(x, *others):
    return lax.optimization_barrier((x, *others))[0]


def scale_pair_kernel(gate_ref, up_ref, gate_s_ref, up_s_ref, out_ref):
    units = gate_ref.shape[1]
    for t in range(gate_ref.shape[0] // 128):
        rows = slice(t * 128, (t + 1) * 128)
        for at, ref, s_ref in ((0, gate_ref, gate_s_ref), (units, up_ref, up_s_ref)):
            value = ref[rows, :].astype(jnp.float32) * s_ref[t : t + 1, :]
            out_ref[rows, at : at + units] = value.astype(jnp.bfloat16)


def scale_pair(gate_q, up_q, gate_s, up_s):
    rows, units = gate_q.shape
    block = 1024
    tiles = block // 128
    return pl.pallas_call(
        scale_pair_kernel,
        grid=(rows // block,),
        in_specs=[
            pl.BlockSpec((block, units), lambda i: (i, 0)),
            pl.BlockSpec((block, units), lambda i: (i, 0)),
            pl.BlockSpec((tiles, units), lambda i: (i, 0)),
            pl.BlockSpec((tiles, units), lambda i: (i, 0)),
        ],
        out_specs=pl.BlockSpec((block, 2 * units), lambda i: (i, 0)),
        out_shape=jax.ShapeDtypeStruct((rows, 2 * units), jnp.bfloat16),
        compiler_params=pltpu.CompilerParams(vmem_limit_bytes=40 * 1024 * 1024),
        cost_estimate=pl.CostEstimate(
            flops=2 * rows * units, bytes_accessed=8 * rows * units, transcendentals=0
        ),
    )(gate_q, up_q, jnp.repeat(gate_s, 128, axis=1), jnp.repeat(up_s, 128, axis=1))


def scale_one_kernel(q_ref, s_ref, out_ref):
    for t in range(q_ref.shape[0] // 128):
        rows = slice(t * 128, (t + 1) * 128)
        value = q_ref[rows, :].astype(jnp.float32) * s_ref[t : t + 1, :]
        out_ref[rows, :] = value.astype(jnp.bfloat16)


def scale_one(q, s):
    rows, cols = q.shape
    block = 1024
    return pl.pallas_call(
        scale_one_kernel,
        grid=(cols // block,),
        in_specs=[
            pl.BlockSpec((rows, block), lambda i: (0, i)),
            pl.BlockSpec((rows // 128, block), lambda i: (0, i)),
        ],
        out_specs=pl.BlockSpec((rows, block), lambda i: (0, i)),
        out_shape=jax.ShapeDtypeStruct((rows, cols), jnp.bfloat16),
        compiler_params=pltpu.CompilerParams(vmem_limit_bytes=40 * 1024 * 1024),
        cost_estimate=pl.CostEstimate(
            flops=rows * cols, bytes_accessed=4 * rows * cols, transcendentals=0
        ),
    )(q, jnp.repeat(s, 128, axis=1))


def gather_ring(block, outer):
    from_left = ring(block, outer, 1)
    from_right = ring(block, outer, -1)
    far_a = ring(from_left[:1], outer, 1)
    far_b = ring(from_right[1:], outer, -1)
    return from_left, from_right, far_a, far_b


def f32(x):
    return x.astype(jnp.float32)


def bf16(x):
    return x.astype(jnp.bfloat16)


def reduce_ring(terms, outer):
    own, right, left, far = terms
    got_a = ring(far[0], outer, 1)
    got_b = ring(far[1], outer, -1)
    to_right = jnp.stack([bf16(f32(right[0]) + f32(got_a)), right[1]])
    to_left = jnp.stack([left[0], bf16(f32(left[1]) + f32(got_b))])
    from_left = ring(to_right, outer, 1)
    from_right = ring(to_left, outer, -1)
    return [
        bf16(f32(own[h]) + f32(from_left[h]) + f32(from_right[h])) for h in range(2)
    ]


def local(tokens, gate_q, gate_scale, up_q, up_scale, down_q, down_scale):
    width = tokens.shape[1]
    units = gate_q.shape[1]
    n = tokens.shape[0] // (CHUNKS * 4)
    xl = lax.axis_index("xl")
    c = lax.axis_index("c")

    gate_up_w = scale_pair(gate_q, up_q, gate_scale, up_scale)
    down_w = scale_one(down_q, down_scale)

    t = tokens.reshape(CHUNKS, 2, 2, n, width)
    t = jnp.where(xl == 1, t[:, ::-1], t)
    t = jnp.where(c == 1, t[:, :, ::-1], t)
    t = t.transpose(0, 2, 1, 3, 4)

    def gather(k, block, wait):
        pair = jnp.stack([block, swap(block, "xh")])
        left, right, far_a, far_b = gather_ring(pair, False)
        far = jnp.concatenate([far_a, far_b])
        plane = jnp.stack([pair, right, left, far], axis=3)
        if wait is not None:
            plane = after(plane, wait)
        left, right, far_a, far_b = gather_ring(plane, True)
        whole = [
            jnp.stack([plane[0], right[0], left[0], far_a[0]], axis=2),
            jnp.stack([plane[1], right[1], left[1], far_b[0]], axis=2),
        ]
        return whole, left

    def middle(rows):
        part = bf16(
            jnp.dot(rows.reshape(-1, width), gate_up_w, preferred_element_type=jnp.float32)
        ).reshape(2, 2, 4, 4, n, 2 * units)
        other = swap(part[1], "c").transpose(0, 2, 1, 3, 4)
        away = swap(bf16(f32(part[0, 1]) + f32(other[1])), "xl")
        total = f32(part[0, 0]) + f32(other[0]) + f32(away)
        hidden = bf16(jax.nn.silu(total[..., :units]) * total[..., units:])
        near = jnp.stack([hidden, swap(hidden, "xl")])
        hid = jnp.stack([near, swap(near, "c").transpose(0, 2, 1, 3, 4)])
        hid = hid.transpose(2, 0, 1, 3, 4, 5)
        out = bf16(
            jnp.dot(hid.reshape(-1, units), down_w, preferred_element_type=jnp.float32)
        )
        return out.reshape(4, 4, 4, n, width)

    def scatter(outs):
        plane = reduce_ring([[outs[h][o] for h in range(2)] for o in range(4)], True)
        line = reduce_ring([[plane[h][:, i] for h in range(2)] for i in range(4)], False)
        return f32(line[0]) + f32(swap(line[1], "xh"))

    wholes = []
    wait = None
    for k in range(CHUNKS):
        whole, wait = gather(k, t[k], wait)
        wholes.append(whole)
    results = []
    for k in range(CHUNKS):
        outs = [middle(rows) for rows in wholes[k]]
        results.append(scatter(outs))
    t = bf16(jnp.stack(results)).reshape(CHUNKS, 2, 2, n, width)
    t = t.transpose(0, 2, 1, 3, 4)
    t = jnp.where(c == 1, t[:, :, ::-1], t)
    t = jnp.where(xl == 1, t[:, ::-1], t)
    return t.reshape(tokens.shape)


def solution(mesh):
    fine = Mesh(mesh.devices.reshape(SIZES), AXES)
    gx, gy = ("z", "y", "xh"), ("xl", "c")
    placed = (
        P(gx, gy),
        P(gy, gx),
        P(gy, gx),
        P(gy, gx),
        P(gy, gx),
        P(gx, gy),
        P(gx, gy),
    )
    return jax.shard_map(
        local, mesh=fine, in_specs=placed, out_specs=P(gx, gy), check_vma=False
    )
```

```python
import functools

import jax
import jax.numpy as jnp
from jax import lax
from jax.experimental import pallas as pl
from jax.experimental.pallas import tpu as pltpu
from jax.sharding import Mesh
from jax.sharding import PartitionSpec as P

AXES = ("z", "y", "xh", "xl", "c")
SIZES = (4, 4, 2, 2, 2)


def index_of(z, y, xh, xl, c):
    return (((z * 4 + y) * 2 + xh) * 2 + xl) * 2 + c


def every_device():
    for z in range(4):
        for y in range(4):
            for xh in range(2):
                for xl in range(2):
                    for c in range(2):
                        yield z, y, xh, xl, c


def ring_pairs(outer, step):
    pairs = []
    for z, y, xh, xl, c in every_device():
        if (c == 0) == outer:
            there = ((z + step) % 4, y, xh, xl, c)
        else:
            there = (z, (y + step) % 4, xh, xl, c)
        pairs.append((index_of(z, y, xh, xl, c), index_of(*there)))
    return pairs


def ring(x, outer, step):
    return lax.ppermute(x, AXES, ring_pairs(outer, step))


def swap(x, axis):
    return lax.ppermute(x, axis, [(0, 1), (1, 0)])


def scale_pair_kernel(gate_ref, up_ref, gate_s_ref, up_s_ref, *out_refs):
    for t in range(gate_ref.shape[0] // 128):
        rows = slice(t * 128, (t + 1) * 128)
        for at, (ref, s_ref) in enumerate(((gate_ref, gate_s_ref), (up_ref, up_s_ref))):
            value = (ref[rows, :].astype(jnp.float32) * s_ref[t : t + 1, :]).astype(jnp.bfloat16)
            first = 0
            for out_ref in out_refs:
                units = out_ref.shape[1] // 2
                out_ref[rows, at * units : (at + 1) * units] = value[:, first : first + units]
                first += units


def scale_pair(gate_q, up_q, gate_s, up_s, groups):
    rows, units = gate_q.shape
    block = 1024
    tiles = block // 128
    return pl.pallas_call(
        scale_pair_kernel,
        grid=(rows // block,),
        in_specs=[
            pl.BlockSpec((block, units), lambda i: (i, 0)),
            pl.BlockSpec((block, units), lambda i: (i, 0)),
            pl.BlockSpec((tiles, units), lambda i: (i, 0)),
            pl.BlockSpec((tiles, units), lambda i: (i, 0)),
        ],
        out_specs=[pl.BlockSpec((block, 2 * g), lambda i: (i, 0)) for g in groups],
        out_shape=[jax.ShapeDtypeStruct((rows, 2 * g), jnp.bfloat16) for g in groups],
        compiler_params=pltpu.CompilerParams(vmem_limit_bytes=40 * 1024 * 1024),
        cost_estimate=pl.CostEstimate(
            flops=2 * rows * units, bytes_accessed=8 * rows * units, transcendentals=0
        ),
    )(gate_q, up_q, jnp.repeat(gate_s, 128, axis=1), jnp.repeat(up_s, 128, axis=1))


def scale_one_kernel(q_ref, s_ref, out_ref):
    for t in range(q_ref.shape[0] // 128):
        rows = slice(t * 128, (t + 1) * 128)
        value = q_ref[rows, :].astype(jnp.float32) * s_ref[t : t + 1, :]
        out_ref[rows, :] = value.astype(jnp.bfloat16)


def scale_one(q, s):
    rows, cols = q.shape
    block = 1024
    return pl.pallas_call(
        scale_one_kernel,
        grid=(cols // block,),
        in_specs=[
            pl.BlockSpec((rows, block), lambda i: (0, i)),
            pl.BlockSpec((rows // 128, block), lambda i: (0, i)),
        ],
        out_specs=pl.BlockSpec((rows, block), lambda i: (0, i)),
        out_shape=jax.ShapeDtypeStruct((rows, cols), jnp.bfloat16),
        compiler_params=pltpu.CompilerParams(vmem_limit_bytes=40 * 1024 * 1024),
        cost_estimate=pl.CostEstimate(
            flops=rows * cols, bytes_accessed=4 * rows * cols, transcendentals=0
        ),
    )(q, jnp.repeat(s, 128, axis=1))


def f32(x):
    return x.astype(jnp.float32)


def bf16(x):
    return x.astype(jnp.bfloat16)


def together(*arrays):
    return lax.optimization_barrier(arrays)


def gather_direct(block, outer):
    return [block] + [ring(block, outer, step) for step in (-1, 2, 1)]


def scatter_direct(terms, outer):
    return [terms[0]] + [ring(terms[d], outer, step) for d, step in ((1, 1), (2, 2), (3, -1))]


def total_of(terms):
    return functools.reduce(jnp.add, (f32(t) for t in terms))


def up_kernel(places, count, *refs):
    pieces, w_ref, keep_ref, send_ref, x, sems = refs[:count], *refs[count:]
    rows = pieces[0].shape[3]
    quarter = x.shape[0] // 4
    half = keep_ref.shape[0]

    def copies(q):
        return [
            pltpu.make_async_copy(
                pieces[i].at[at, q // 2, q % 2],
                x.at[pl.ds(q * quarter + k * rows, rows), :],
                sems.at[q * len(places) + k],
            )
            for k, (i, at) in enumerate(places)
        ]

    def put(q, value):
        ref = (keep_ref, send_ref)[q // 2]
        ref[q % 2 * quarter : (q % 2 + 1) * quarter, :] = value.astype(jnp.bfloat16)

    @pl.when(pl.program_id(0) == 0)
    def _():
        for q in range(4):
            for copy in copies(q):
                copy.start()
        for q in range(4):
            for copy in copies(q):
                copy.wait()
            put(
                q,
                jnp.dot(
                    x[q * quarter : (q + 1) * quarter, :],
                    w_ref[...],
                    preferred_element_type=jnp.float32,
                ),
            )

    @pl.when(pl.program_id(0) != 0)
    def _():
        part = jnp.dot(x[...], w_ref[...], preferred_element_type=jnp.float32)
        keep_ref[...] = part[:half].astype(jnp.bfloat16)
        send_ref[...] = part[half:].astype(jnp.bfloat16)


def up_part(pieces, w):
    arrays, places = [], [None] * 8
    for outer, piece in enumerate(pieces):
        if isinstance(piece, list):
            for s in range(2):
                places[s * 4 + outer] = (len(arrays), 0)
                arrays.append(piece[s])
        else:
            for s in range(2):
                places[s * 4 + outer] = (len(arrays), s)
            arrays.append(piece)
    rows, width = arrays[0].shape[3:]
    columns = w.shape[1]
    block = 256
    outs = pl.pallas_call(
        functools.partial(up_kernel, places, len(arrays)),
        grid=(columns // block,),
        in_specs=[pl.BlockSpec(memory_space=pl.ANY)] * len(arrays)
        + [pl.BlockSpec((width, block), lambda j: (0, j))],
        out_specs=[pl.BlockSpec((16 * rows, block), lambda j: (0, j))] * 2,
        out_shape=[jax.ShapeDtypeStruct((16 * rows, columns), jnp.bfloat16)] * 2,
        scratch_shapes=[
            pltpu.VMEM((32 * rows, width), jnp.bfloat16),
            pltpu.SemaphoreType.DMA((32,)),
        ],
        compiler_params=pltpu.CompilerParams(vmem_limit_bytes=40 * 1024 * 1024),
        cost_estimate=pl.CostEstimate(flops=1, bytes_accessed=1, transcendentals=0),
    )(*arrays, w)
    return [o.reshape(2, 2, 4, rows, columns) for o in outs]


def down_kernel(x_ref, w_ref, *out_refs):
    out = jnp.dot(x_ref[...], w_ref[...], preferred_element_type=jnp.float32)
    first = 0
    for ref in out_refs:
        rows = ref.shape[0]
        ref[...] = out[first : first + rows].astype(jnp.bfloat16)
        first += rows


def down_part(x, w, sizes):
    rows, units = x.shape
    width = w.shape[1]
    block = 1024
    return pl.pallas_call(
        down_kernel,
        grid=(width // block,),
        in_specs=[
            pl.BlockSpec((rows, units), lambda j: (0, 0)),
            pl.BlockSpec((units, block), lambda j: (0, j)),
        ],
        out_specs=[pl.BlockSpec((size, block), lambda j: (0, j)) for size in sizes],
        out_shape=[jax.ShapeDtypeStruct((size, width), jnp.bfloat16) for size in sizes],
        compiler_params=pltpu.CompilerParams(vmem_limit_bytes=40 * 1024 * 1024),
        cost_estimate=pl.CostEstimate(flops=1, bytes_accessed=1, transcendentals=0),
    )(x, w)


def local(tokens, gate_q, gate_scale, up_q, up_scale, down_q, down_scale):
    width = tokens.shape[1]
    units = gate_q.shape[1]
    first = units // 128 // 2 * 128
    groups = (first, units - first)
    n = tokens.shape[0] // 8
    slot = 2 * 4 * 4 * n
    xl = lax.axis_index("xl")
    c = lax.axis_index("c")

    t = tokens.reshape(2, 2, 2, n, width)
    t = jnp.where(xl == 1, t[:, ::-1], t)
    t = jnp.where(c == 1, t[:, :, ::-1], t)
    t = t.transpose(0, 2, 1, 3, 4)

    def plane_of(block):
        return jnp.stack(gather_direct(block, False), axis=3).reshape(2, 2, 2, 4 * n, width)

    def other_core(x):
        shape = x.shape
        x = swap(x, "c").reshape(2, 2, 4, 4, n, shape[-1])
        return x.transpose(0, 1, 3, 2, 4, 5).reshape(shape)

    def first_sum(keep, send):
        other = other_core(send)
        return f32(keep[0]) + f32(other[0]), bf16(f32(keep[1]) + f32(other[1]))

    def activate(stay, got, g):
        total = stay + f32(got)
        return bf16(jax.nn.silu(total[..., :g]) * total[..., g:])

    def hidden_rows(halves):
        near = jnp.concatenate([jnp.stack(h) for h in halves], axis=-1)
        hid = jnp.stack([near, other_core(near)])
        return hid.transpose(3, 2, 0, 1, 4, 5).reshape(4, slot, units)

    def down_far(hid):
        return down_part(hid[2], down_w, (slot // 2,) * 2)

    def down_near(hid):
        x = jnp.concatenate([hid[1], hid[3], hid[0]])
        outs = down_part(x, down_w, (slot // 2,) * 4 + (slot,))
        return outs[0:2], outs[2:4], outs[4]

    def relay(far):
        return ring(far[0], True, 1), ring(far[1], True, -1)

    def join(got, right, left):
        return (
            jnp.concatenate([bf16(f32(right[0]) + f32(got[0])), right[1]]),
            jnp.concatenate([left[0], bf16(f32(left[1]) + f32(got[1]))]),
        )

    def by_inner(terms):
        terms = [x.reshape(2, 4, 4, n, width) for x in terms]
        return [total_of([x[:, :, i] for x in terms]) for i in range(4)]

    def scatter_inner(terms):
        return total_of(scatter_direct([terms[0]] + [bf16(x) for x in terms[1:]], False))

    partner = swap(t, "xh")
    plane1 = plane_of(t)
    partner, plane1 = together(partner, plane1)
    plane0 = plane_of(partner)
    plane0, gate_q, up_q, down_q = together(plane0, gate_q, up_q, down_q)
    left, right = ring(plane0, True, 1), ring(plane0, True, -1)
    w0, w1 = scale_pair(gate_q, up_q, gate_scale, up_scale, groups)
    down_w = scale_one(down_q, down_scale)
    left, right, w0, w1, down_w = together(left, right, w0, w1, down_w)
    far_a, far_b = ring(left[:1], True, 1), ring(right[1:], True, -1)

    plane1, far_a, far_b = together(plane1, far_a, far_b)
    pieces0 = [plane0, right, [far_a, far_b], left]
    left, right = ring(plane1, True, 1), ring(plane1, True, -1)

    keep, send = up_part(pieces0, w0)
    stay0, away0 = first_sum(keep, send)
    away0, pieces0[0] = together(away0, pieces0[0])
    got0 = swap(away0, "xl")
    keep, send = up_part(pieces0, w1)
    send, got0, left, right = together(send, got0, left, right)
    far_a, far_b = ring(left[:1], True, 1), ring(right[1:], True, -1)
    stay1, away1 = first_sum(keep, send)
    got1 = swap(away1, "xl")
    hid0 = activate(stay0, got0, groups[0])
    hid0 = (hid0, swap(hid0, "xl"))

    pieces1 = [plane1, right, [far_a, far_b], left]
    hid1 = activate(stay1, got1, groups[1])
    hid1, pieces1[0] = together(hid1, pieces1[0])
    keep, send = up_part(pieces1, w0)
    next_stay0, next_away0 = first_sum(keep, send)

    hid1, other1 = together(hid1, swap(hid1, "xl"), send)[:2]
    hid = hidden_rows((hid0, (hid1, other1)))
    hid, next_away0 = together(hid, next_away0)
    next_got0 = swap(next_away0, "xl")
    far = down_far(hid)
    hid, *far = together(hid, *far)
    got = relay(far)
    right, left, own = down_near(hid)
    own, *got = together(own, *got)
    to_right, to_left = join(got, right, left)
    to_right, to_left, pieces1[0] = together(to_right, to_left, pieces1[0])
    from_left, from_right = ring(to_right, True, 1), ring(to_left, True, -1)

    keep, send = up_part(pieces1, w1)
    send, next_got0 = together(send, next_got0)
    stay1, away1 = first_sum(keep, send)
    got1 = swap(away1, "xl")
    hid0 = activate(next_stay0, next_got0, groups[0])
    other0, from_left, from_right = together(swap(hid0, "xl"), from_left, from_right)
    hid0 = (hid0, other0)

    sums = bf16(scatter_inner(by_inner([own, from_left, from_right])))

    hid1 = activate(stay1, got1, groups[1])
    hid1 = (hid1, swap(hid1, "xl"))
    hid, sums = together(hidden_rows((hid0, hid1)), sums)
    crossing = swap(sums, "xh")
    far = down_far(hid)
    hid, *far = together(hid, *far)
    got = relay(far)
    right, left, own = down_near(hid)
    own, crossing, *got = together(own, crossing, *got)
    to_right, to_left = together(*join(got, right, left))
    from_left, from_right = ring(to_right, True, 1), ring(to_left, True, -1)
    from_left, from_right = together(from_left, from_right)
    t = scatter_inner(by_inner([own, from_left, from_right])) + f32(crossing)

    t = bf16(t).reshape(2, 2, 2, n, width).transpose(0, 2, 1, 3, 4)
    t = jnp.where(c == 1, t[:, :, ::-1], t)
    t = jnp.where(xl == 1, t[:, ::-1], t)
    return t.reshape(tokens.shape)


def solution(mesh):
    fine = Mesh(mesh.devices.reshape(SIZES), AXES)
    gx, gy = ("z", "y", "xh"), ("xl", "c")
    placed = (
        P(gx, gy),
        P(gy, gx),
        P(gy, gx),
        P(gy, gx),
        P(gy, gx),
        P(gx, gy),
        P(gx, gy),
    )
    return jax.shard_map(
        local, mesh=fine, in_specs=placed, out_specs=P(gx, gy), check_vma=False
    )
```

```python
import functools

import jax
import jax.numpy as jnp
from jax import lax
from jax.experimental import pallas as pl
from jax.experimental.pallas import tpu as pltpu
from jax.sharding import Mesh
from jax.sharding import PartitionSpec as P

AXES = ("z", "y", "xh", "xl", "c")
SIZES = (4, 4, 2, 2, 2)


def index_of(z, y, xh, xl, c):
    return (((z * 4 + y) * 2 + xh) * 2 + xl) * 2 + c


def every_device():
    for z in range(4):
        for y in range(4):
            for xh in range(2):
                for xl in range(2):
                    for c in range(2):
                        yield z, y, xh, xl, c


def ring_pairs(outer, step):
    pairs = []
    for z, y, xh, xl, c in every_device():
        if (c == 0) == outer:
            there = ((z + step) % 4, y, xh, xl, c)
        else:
            there = (z, (y + step) % 4, xh, xl, c)
        pairs.append((index_of(z, y, xh, xl, c), index_of(*there)))
    return pairs


def ring(x, outer, step):
    return lax.ppermute(x, AXES, ring_pairs(outer, step))


def swap(x, axis):
    return lax.ppermute(x, axis, [(0, 1), (1, 0)])


def scale_pair_kernel(gate_ref, up_ref, gate_s_ref, up_s_ref, *out_refs):
    for t in range(gate_ref.shape[0] // 128):
        rows = slice(t * 128, (t + 1) * 128)
        for at, (ref, s_ref) in enumerate(((gate_ref, gate_s_ref), (up_ref, up_s_ref))):
            value = (ref[rows, :].astype(jnp.float32) * s_ref[t : t + 1, :]).astype(jnp.bfloat16)
            first = 0
            for out_ref in out_refs:
                units = out_ref.shape[1] // 2
                out_ref[rows, at * units : (at + 1) * units] = value[:, first : first + units]
                first += units


def scale_pair(gate_q, up_q, gate_s, up_s, groups):
    rows, units = gate_q.shape
    block = 1024
    tiles = block // 128
    return pl.pallas_call(
        scale_pair_kernel,
        grid=(rows // block,),
        in_specs=[
            pl.BlockSpec((block, units), lambda i: (i, 0)),
            pl.BlockSpec((block, units), lambda i: (i, 0)),
            pl.BlockSpec((tiles, units), lambda i: (i, 0)),
            pl.BlockSpec((tiles, units), lambda i: (i, 0)),
        ],
        out_specs=[pl.BlockSpec((block, 2 * g), lambda i: (i, 0)) for g in groups],
        out_shape=[jax.ShapeDtypeStruct((rows, 2 * g), jnp.bfloat16) for g in groups],
        compiler_params=pltpu.CompilerParams(vmem_limit_bytes=40 * 1024 * 1024),
        cost_estimate=pl.CostEstimate(
            flops=2 * rows * units, bytes_accessed=8 * rows * units, transcendentals=0
        ),
    )(gate_q, up_q, jnp.repeat(gate_s, 128, axis=1), jnp.repeat(up_s, 128, axis=1))


def scale_one_kernel(q_ref, s_ref, out_ref):
    for t in range(q_ref.shape[0] // 128):
        rows = slice(t * 128, (t + 1) * 128)
        value = q_ref[rows, :].astype(jnp.float32) * s_ref[t : t + 1, :]
        out_ref[rows, :] = value.astype(jnp.bfloat16)


def scale_one(q, s):
    rows, cols = q.shape
    block = 1024
    return pl.pallas_call(
        scale_one_kernel,
        grid=(cols // block,),
        in_specs=[
            pl.BlockSpec((rows, block), lambda i: (0, i)),
            pl.BlockSpec((rows // 128, block), lambda i: (0, i)),
        ],
        out_specs=pl.BlockSpec((rows, block), lambda i: (0, i)),
        out_shape=jax.ShapeDtypeStruct((rows, cols), jnp.bfloat16),
        compiler_params=pltpu.CompilerParams(vmem_limit_bytes=40 * 1024 * 1024),
        cost_estimate=pl.CostEstimate(
            flops=rows * cols, bytes_accessed=4 * rows * cols, transcendentals=0
        ),
    )(q, jnp.repeat(s, 128, axis=1))


def f32(x):
    return x.astype(jnp.float32)


def bf16(x):
    return x.astype(jnp.bfloat16)


def together(*arrays):
    return lax.optimization_barrier(arrays)


def gather_direct(block, outer):
    return [block] + [ring(block, outer, step) for step in (-1, 2, 1)]


def scatter_direct(terms, outer):
    return [terms[0]] + [ring(terms[d], outer, step) for d, step in ((1, 1), (2, 2), (3, -1))]


def total_of(terms):
    return functools.reduce(jnp.add, (f32(t) for t in terms))


def up_kernel(parts, count, given, *refs):
    pieces, w_ref, x, sems = refs[:count], refs[count], refs[-2], refs[-1]
    outs = refs[count + 1 + given : -2]
    rows = pieces[0].shape[3]

    def copies(blocks, first):
        return [
            pltpu.make_async_copy(
                pieces[i].at[s, dc, dxl],
                x.at[pl.ds((first + k) * rows, rows), :],
                sems.at[first + k],
            )
            for k, (i, s, dc, dxl) in enumerate(blocks)
        ]

    def each():
        first = 0
        for out, at, blocks in parts:
            yield out, at * rows, blocks, first
            first += len(blocks)

    def put(out, at, value):
        outs[out][at : at + value.shape[0], :] = value.astype(jnp.bfloat16)

    def times(first, last):
        return jnp.dot(
            x[first * rows : last * rows, :], w_ref[...], preferred_element_type=jnp.float32
        )

    @pl.when(pl.program_id(0) == 0)
    def _():
        for _, _, blocks, first in each():
            for copy in copies(blocks, first):
                copy.start()
        for out, at, blocks, first in each():
            for copy in copies(blocks, first):
                copy.wait()
            put(out, at, times(first, first + len(blocks)))

    @pl.when(pl.program_id(0) != 0)
    def _():
        part = times(0, x.shape[0] // rows)
        for out, at, blocks, first in each():
            put(out, at, part[first * rows : (first + len(blocks)) * rows])


def up_part(pieces, w, into=None):
    arrays, places = [], []
    for piece in pieces:
        if isinstance(piece, list):
            places.append([(len(arrays) + s, 0) for s in range(2)])
            arrays.extend(piece)
        else:
            places.append([(len(arrays), s) for s in range(2)])
            arrays.append(piece)
    parts = []
    for dc in range(2):
        for at in range(0, len(places), 2):
            blocks = [
                (i, s, dc, dxl)
                for place in places[at : at + 2]
                for dxl in range(2)
                for i, s in place
            ]
            parts.append((dc, 4 * at, blocks))
    rows, width = arrays[0].shape[3:]
    columns = w.shape[1]
    block = 256
    count = 4 * len(pieces)
    given = [] if into is None else [o.reshape(16 * rows, columns) for o in into]
    place = 0 if into is None else 4 - len(pieces)
    outs = pl.pallas_call(
        functools.partial(up_kernel, parts, len(arrays), len(given)),
        grid=(columns // block,),
        in_specs=[pl.BlockSpec(memory_space=pl.ANY)] * len(arrays)
        + [pl.BlockSpec((width, block), lambda j: (0, j))]
        + [pl.BlockSpec(memory_space=pl.ANY)] * len(given),
        out_specs=[pl.BlockSpec((count * rows, block), lambda j: (place, j))] * 2,
        out_shape=[jax.ShapeDtypeStruct((16 * rows, columns), jnp.bfloat16)] * 2,
        scratch_shapes=[
            pltpu.VMEM((2 * count * rows, width), jnp.bfloat16),
            pltpu.SemaphoreType.DMA((2 * count,)),
        ],
        input_output_aliases={len(arrays) + 1 + i: i for i in range(len(given))},
        compiler_params=pltpu.CompilerParams(vmem_limit_bytes=40 * 1024 * 1024),
        cost_estimate=pl.CostEstimate(flops=1, bytes_accessed=1, transcendentals=0),
    )(*arrays, w, *given)
    return [o.reshape(4, 2, 2, rows, columns) for o in outs]


def down_kernel(x_ref, w_ref, *out_refs):
    out = jnp.dot(x_ref[...], w_ref[...], preferred_element_type=jnp.float32)
    first = 0
    for ref in out_refs:
        rows = ref.shape[0]
        ref[...] = out[first : first + rows].astype(jnp.bfloat16)
        first += rows


def down_part(x, w, sizes):
    rows, units = x.shape
    width = w.shape[1]
    block = 1024
    return pl.pallas_call(
        down_kernel,
        grid=(width // block,),
        in_specs=[
            pl.BlockSpec((rows, units), lambda j: (0, 0)),
            pl.BlockSpec((units, block), lambda j: (0, j)),
        ],
        out_specs=[pl.BlockSpec((size, block), lambda j: (0, j)) for size in sizes],
        out_shape=[jax.ShapeDtypeStruct((size, width), jnp.bfloat16) for size in sizes],
        compiler_params=pltpu.CompilerParams(vmem_limit_bytes=40 * 1024 * 1024),
        cost_estimate=pl.CostEstimate(flops=1, bytes_accessed=1, transcendentals=0),
    )(x, w)


def local(tokens, gate_q, gate_scale, up_q, up_scale, down_q, down_scale):
    width = tokens.shape[1]
    units = gate_q.shape[1]
    first = (units // 128 + 1) // 2 * 128
    groups = (first, units - first)
    n = tokens.shape[0] // 8
    slot = 2 * 4 * 4 * n
    xl = lax.axis_index("xl")
    c = lax.axis_index("c")

    t = tokens.reshape(2, 2, 2, n, width)
    t = jnp.where(xl == 1, t[:, ::-1], t)
    t = jnp.where(c == 1, t[:, :, ::-1], t)
    t = t.transpose(0, 2, 1, 3, 4)

    def plane_of(block):
        own, right, far, left = gather_direct(block, False)
        return jnp.stack([own, right, left, far], axis=3).reshape(2, 2, 2, 4 * n, width)

    def other_core(x):
        shape = x.shape
        x = swap(x, "c").reshape(4, -1, 4, n, shape[-1])
        return x.transpose(2, 1, 0, 3, 4).reshape(shape)

    def first_sum(keep, send):
        other = other_core(send)
        return (
            f32(keep[:, 0]) + f32(other[:, 0]),
            bf16(f32(keep[:, 1]) + f32(other[:, 1])),
        )

    def activate(stay, got, g):
        total = stay + f32(got)
        return bf16(jax.nn.silu(total[..., :g]) * total[..., g:])

    def hidden_rows(halves):
        near = jnp.concatenate([jnp.stack(h, axis=2) for h in halves], axis=-1)
        hid = jnp.stack([near, other_core(near)], axis=2)
        return hid.reshape(4, slot, units)

    def down_far(hid):
        return down_part(hid[3], down_w, (slot // 2,) * 2)

    def down_near(hid):
        outs = down_part(hid[:3].reshape(-1, units), down_w, (slot,) + (slot // 2,) * 4)
        return outs[1:3], outs[3:5], outs[0]

    def relay(far):
        return ring(far[0], True, 1), ring(far[1], True, -1)

    def join(got, right, left):
        return (
            jnp.concatenate([bf16(f32(right[0]) + f32(got[0])), right[1]]),
            jnp.concatenate([left[0], bf16(f32(left[1]) + f32(got[1]))]),
        )

    def by_inner(terms):
        terms = [x.reshape(2, 4, 4, n, width) for x in terms]
        return [total_of([x[:, :, i] for x in terms]) for i in range(4)]

    def scatter_inner(terms):
        own, right, left, far = terms
        return total_of(scatter_direct([own] + [bf16(x) for x in (right, far, left)], False))

    partner = swap(t, "xh")
    plane1 = plane_of(t)
    partner, plane1 = together(partner, plane1)
    plane0 = plane_of(partner)
    plane0, gate_q, up_q, down_q = together(plane0, gate_q, up_q, down_q)
    left, right = ring(plane0, True, 1), ring(plane0, True, -1)
    w0, w1 = scale_pair(gate_q, up_q, gate_scale, up_scale, groups)
    down_w = scale_one(down_q, down_scale)
    left, right, w0, w1, down_w = together(left, right, w0, w1, down_w)
    far_a, far_b = ring(left[:1], True, 1), ring(right[1:], True, -1)

    pieces0 = [plane0, right, left]
    sums0 = up_part(pieces0, w0)

    plane1, far_a, far_b, *sums0 = together(plane1, far_a, far_b, *sums0)
    pieces0.append([far_a, far_b])
    left, right = ring(plane1, True, 1), ring(plane1, True, -1)

    keep, send = up_part(pieces0[3:], w0, sums0)
    stay0, away0 = first_sum(keep, send)
    away0, pieces0[0] = together(away0, pieces0[0])
    got0 = swap(away0, "xl")
    keep, send = up_part(pieces0, w1)
    send, got0, left, right = together(send, got0, left, right)
    far_a, far_b = ring(left[:1], True, 1), ring(right[1:], True, -1)
    stay1, away1 = first_sum(keep, send)
    got1 = swap(away1, "xl")
    hid0 = activate(stay0, got0, groups[0])
    other0 = swap(hid0, "xl")

    pieces1 = [plane1, right, left]
    sums1 = up_part(pieces1, w0)
    got1, other0, *sums1 = together(got1, other0, *sums1)
    hid0 = (hid0, other0)

    hid1 = activate(stay1, got1, groups[1])
    hid1, far_a, far_b = together(hid1, far_a, far_b)
    pieces1.append([far_a, far_b])
    keep, send = up_part(pieces1[3:], w0, sums1)
    next_stay0, next_away0 = first_sum(keep, send)

    hid1, other1 = together(hid1, swap(hid1, "xl"), send)[:2]
    hid = hidden_rows((hid0, (hid1, other1)))
    hid, next_away0 = together(hid, next_away0)
    next_got0 = swap(next_away0, "xl")
    far = down_far(hid)
    hid, *far = together(hid, *far)
    got = relay(far)
    right, left, own = down_near(hid)
    own, *got = together(own, *got)
    to_right, to_left = join(got, right, left)
    to_right, to_left, pieces1[0] = together(to_right, to_left, pieces1[0])
    from_left, from_right = ring(to_right, True, 1), ring(to_left, True, -1)

    keep, send = up_part(pieces1, w1)
    send, next_got0 = together(send, next_got0)
    stay1, away1 = first_sum(keep, send)
    got1 = swap(away1, "xl")
    hid0 = activate(next_stay0, next_got0, groups[0])
    other0, from_left, from_right = together(swap(hid0, "xl"), from_left, from_right)
    hid0 = (hid0, other0)

    sums = bf16(scatter_inner(by_inner([own, from_left, from_right])))

    hid1 = activate(stay1, got1, groups[1])
    hid1 = (hid1, swap(hid1, "xl"))
    hid = hidden_rows((hid0, hid1))
    far = down_far(hid)
    hid, *far = together(hid, *far)
    got = relay(far)
    right, left, own = down_near(hid)
    own, sums, *got = together(own, sums, *got)
    crossing = swap(sums, "xh")
    to_right, to_left = together(*join(got, right, left))
    from_left, from_right = ring(to_right, True, 1), ring(to_left, True, -1)
    from_left, from_right, crossing = together(from_left, from_right, crossing)
    t = scatter_inner(by_inner([own, from_left, from_right])) + f32(crossing)

    t = bf16(t).reshape(2, 2, 2, n, width).transpose(0, 2, 1, 3, 4)
    t = jnp.where(c == 1, t[:, :, ::-1], t)
    t = jnp.where(xl == 1, t[:, ::-1], t)
    return t.reshape(tokens.shape)


def solution(mesh):
    fine = Mesh(mesh.devices.reshape(SIZES), AXES)
    gx, gy = ("z", "y", "xh"), ("xl", "c")
    placed = (
        P(gx, gy),
        P(gy, gx),
        P(gy, gx),
        P(gy, gx),
        P(gy, gx),
        P(gx, gy),
        P(gx, gy),
    )
    return jax.shard_map(
        local, mesh=fine, in_specs=placed, out_specs=P(gx, gy), check_vma=False
    )
```

```python
import functools

import jax
import jax.numpy as jnp
from jax import lax
from jax.experimental import pallas as pl
from jax.experimental.pallas import tpu as pltpu
from jax.sharding import Mesh
from jax.sharding import PartitionSpec as P

AXES = ("z", "y", "xh", "xl", "c")
SIZES = (4, 4, 2, 2, 2)


def index_of(z, y, xh, xl, c):
    return (((z * 4 + y) * 2 + xh) * 2 + xl) * 2 + c


def every_device():
    for z in range(4):
        for y in range(4):
            for xh in range(2):
                for xl in range(2):
                    for c in range(2):
                        yield z, y, xh, xl, c


def ring_pairs(outer, step):
    pairs = []
    for z, y, xh, xl, c in every_device():
        if (c == 0) == outer:
            there = ((z + step) % 4, y, xh, xl, c)
        else:
            there = (z, (y + step) % 4, xh, xl, c)
        pairs.append((index_of(z, y, xh, xl, c), index_of(*there)))
    return pairs


def ring(x, outer, step):
    return lax.ppermute(x, AXES, ring_pairs(outer, step))


def swap(x, axis):
    return lax.ppermute(x, axis, [(0, 1), (1, 0)])


def scale_pair_kernel(gate_ref, up_ref, gate_s_ref, up_s_ref, *out_refs):
    for t in range(gate_ref.shape[0] // 128):
        rows = slice(t * 128, (t + 1) * 128)
        for at, (ref, s_ref) in enumerate(((gate_ref, gate_s_ref), (up_ref, up_s_ref))):
            value = (ref[rows, :].astype(jnp.float32) * s_ref[t : t + 1, :]).astype(jnp.bfloat16)
            first = 0
            for out_ref in out_refs:
                units = out_ref.shape[1] // 2
                out_ref[rows, at * units : (at + 1) * units] = value[:, first : first + units]
                first += units


def scale_pair(gate_q, up_q, gate_s, up_s, groups):
    rows, units = gate_q.shape
    block = 1024
    tiles = block // 128
    return pl.pallas_call(
        scale_pair_kernel,
        grid=(rows // block,),
        in_specs=[
            pl.BlockSpec((block, units), lambda i: (i, 0)),
            pl.BlockSpec((block, units), lambda i: (i, 0)),
            pl.BlockSpec((tiles, units), lambda i: (i, 0)),
            pl.BlockSpec((tiles, units), lambda i: (i, 0)),
        ],
        out_specs=[pl.BlockSpec((block, 2 * g), lambda i: (i, 0)) for g in groups],
        out_shape=[jax.ShapeDtypeStruct((rows, 2 * g), jnp.bfloat16) for g in groups],
        compiler_params=pltpu.CompilerParams(vmem_limit_bytes=40 * 1024 * 1024),
        cost_estimate=pl.CostEstimate(
            flops=2 * rows * units, bytes_accessed=8 * rows * units, transcendentals=0
        ),
    )(gate_q, up_q, jnp.repeat(gate_s, 128, axis=1), jnp.repeat(up_s, 128, axis=1))


def scale_one_kernel(q_ref, s_ref, out_ref):
    for t in range(q_ref.shape[0] // 128):
        rows = slice(t * 128, (t + 1) * 128)
        value = q_ref[rows, :].astype(jnp.float32) * s_ref[t : t + 1, :]
        out_ref[rows, :] = value.astype(jnp.bfloat16)


def scale_one(q, s):
    rows, cols = q.shape
    block = 1024
    return pl.pallas_call(
        scale_one_kernel,
        grid=(cols // block,),
        in_specs=[
            pl.BlockSpec((rows, block), lambda i: (0, i)),
            pl.BlockSpec((rows // 128, block), lambda i: (0, i)),
        ],
        out_specs=pl.BlockSpec((rows, block), lambda i: (0, i)),
        out_shape=jax.ShapeDtypeStruct((rows, cols), jnp.bfloat16),
        compiler_params=pltpu.CompilerParams(vmem_limit_bytes=40 * 1024 * 1024),
        cost_estimate=pl.CostEstimate(
            flops=rows * cols, bytes_accessed=4 * rows * cols, transcendentals=0
        ),
    )(q, jnp.repeat(s, 128, axis=1))


def f32(x):
    return x.astype(jnp.float32)


def bf16(x):
    return x.astype(jnp.bfloat16)


def together(*arrays):
    return lax.optimization_barrier(arrays)


def gather_direct(block, outer):
    return [block] + [ring(block, outer, step) for step in (-1, 2, 1)]


def scatter_direct(terms, outer):
    return [terms[0]] + [ring(terms[d], outer, step) for d, step in ((1, 1), (2, 2), (3, -1))]


def total_of(terms):
    return functools.reduce(jnp.add, (f32(t) for t in terms))


def up_kernel(parts, count, given, *refs):
    pieces, w_ref, x, sems = refs[:count], refs[count], refs[-2], refs[-1]
    outs = refs[count + 1 + given : -2]
    rows = pieces[0].shape[3]

    def copies(blocks, first):
        return [
            pltpu.make_async_copy(
                pieces[i].at[s, dc, dxl],
                x.at[pl.ds((first + k) * rows, rows), :],
                sems.at[first + k],
            )
            for k, (i, s, dc, dxl) in enumerate(blocks)
        ]

    def each():
        first = 0
        for out, at, blocks in parts:
            yield out, at * rows, blocks, first
            first += len(blocks)

    def put(out, at, value):
        outs[out][at : at + value.shape[0], :] = value.astype(jnp.bfloat16)

    def times(first, last):
        return jnp.dot(
            x[first * rows : last * rows, :], w_ref[...], preferred_element_type=jnp.float32
        )

    @pl.when(pl.program_id(0) == 0)
    def _():
        for _, _, blocks, first in each():
            for copy in copies(blocks, first):
                copy.start()
        for out, at, blocks, first in each():
            for copy in copies(blocks, first):
                copy.wait()
            put(out, at, times(first, first + len(blocks)))

    @pl.when(pl.program_id(0) != 0)
    def _():
        part = times(0, x.shape[0] // rows)
        for out, at, blocks, first in each():
            put(out, at, part[first * rows : (first + len(blocks)) * rows])


def up_part(pieces, w, into=None):
    arrays, places = [], []
    for piece in pieces:
        if isinstance(piece, list):
            places.append([(len(arrays) + s, 0) for s in range(2)])
            arrays.extend(piece)
        else:
            places.append([(len(arrays), s) for s in range(2)])
            arrays.append(piece)
    parts = []
    for dc in range(2):
        for at in range(0, len(places), 2):
            blocks = [
                (i, s, dc, dxl)
                for place in places[at : at + 2]
                for dxl in range(2)
                for i, s in place
            ]
            parts.append((dc, 4 * at, blocks))
    rows, width = arrays[0].shape[3:]
    columns = w.shape[1]
    block = 256
    count = 4 * len(pieces)
    given = [] if into is None else [o.reshape(16 * rows, columns) for o in into]
    place = 0 if into is None else 4 - len(pieces)
    outs = pl.pallas_call(
        functools.partial(up_kernel, parts, len(arrays), len(given)),
        grid=(columns // block,),
        in_specs=[pl.BlockSpec(memory_space=pl.ANY)] * len(arrays)
        + [pl.BlockSpec((width, block), lambda j: (0, j))]
        + [pl.BlockSpec(memory_space=pl.ANY)] * len(given),
        out_specs=[pl.BlockSpec((count * rows, block), lambda j: (place, j))] * 2,
        out_shape=[jax.ShapeDtypeStruct((16 * rows, columns), jnp.bfloat16)] * 2,
        scratch_shapes=[
            pltpu.VMEM((2 * count * rows, width), jnp.bfloat16),
            pltpu.SemaphoreType.DMA((2 * count,)),
        ],
        input_output_aliases={len(arrays) + 1 + i: i for i in range(len(given))},
        compiler_params=pltpu.CompilerParams(vmem_limit_bytes=40 * 1024 * 1024),
        cost_estimate=pl.CostEstimate(flops=1, bytes_accessed=1, transcendentals=0),
    )(*arrays, w, *given)
    return [o.reshape(4, 2, 2, rows, columns) for o in outs]


def down_kernel(x_ref, w_ref, *out_refs):
    out = jnp.dot(x_ref[...], w_ref[...], preferred_element_type=jnp.float32)
    first = 0
    for ref in out_refs:
        rows = ref.shape[0]
        ref[...] = out[first : first + rows].astype(jnp.bfloat16)
        first += rows


def down_part(x, w, sizes):
    rows, units = x.shape
    width = w.shape[1]
    block = 1024
    return pl.pallas_call(
        down_kernel,
        grid=(width // block,),
        in_specs=[
            pl.BlockSpec((rows, units), lambda j: (0, 0)),
            pl.BlockSpec((units, block), lambda j: (0, j)),
        ],
        out_specs=[pl.BlockSpec((size, block), lambda j: (0, j)) for size in sizes],
        out_shape=[jax.ShapeDtypeStruct((size, width), jnp.bfloat16) for size in sizes],
        compiler_params=pltpu.CompilerParams(vmem_limit_bytes=40 * 1024 * 1024),
        cost_estimate=pl.CostEstimate(flops=1, bytes_accessed=1, transcendentals=0),
    )(x, w)


def local(tokens, gate_q, gate_scale, up_q, up_scale, down_q, down_scale):
    width = tokens.shape[1]
    units = gate_q.shape[1]
    first = (units // 128 + 1) // 2 * 128
    groups = (first, units - first)
    n = tokens.shape[0] // 8
    slot = 2 * 4 * 4 * n
    half = slot // 2
    xl = lax.axis_index("xl")
    c = lax.axis_index("c")

    def by_distance(t):
        t = t.reshape(2, 2, 2, n, width)
        t = jnp.where(xl == 1, t[:, ::-1], t)
        t = jnp.where(c == 1, t[:, :, ::-1], t)
        return t.transpose(0, 2, 1, 3, 4)

    def plane_of(block):
        own, right, far, left = gather_direct(block, False)
        return jnp.stack([own, right, left, far], axis=3).reshape(2, 2, 2, 4 * n, width)

    def other_core(x):
        shape = x.shape
        x = swap(x, "c").reshape(4, -1, 4, n, shape[-1])
        return x.transpose(2, 1, 0, 3, 4).reshape(shape)

    def first_sum(keep, send):
        other = other_core(send)
        return (
            f32(keep[:, 0]) + f32(other[:, 0]),
            bf16(f32(keep[:, 1]) + f32(other[:, 1])),
        )

    def activate(stay, got, g):
        total = stay + f32(got)
        return bf16(jax.nn.silu(total[..., :g]) * total[..., g:])

    def hidden_rows(halves):
        near = jnp.concatenate([jnp.stack(h, axis=2) for h in halves], axis=-1)
        hid = jnp.stack([near, other_core(near)], axis=2)
        return hid.reshape(4, slot, units)

    def down_first(hid):
        _, right, left, far = hid
        x = jnp.concatenate([far, right[half:], left[:half]])
        outs = list(down_part(x, down_w, (half,) * 4))
        return outs[:2], outs[2:]

    def down_rest(hid):
        own, right, left, _ = hid
        x = jnp.concatenate([own, right[:half], left[half:]])
        outs = list(down_part(x, down_w, (half,) * 4))
        return outs[:2], outs[2:]

    def both_ways(terms):
        return [ring(terms[0], True, 1), ring(terms[1], True, -1)]

    def join(got, rest):
        return [bf16(f32(x) + f32(g)) for x, g in zip(rest, got)]

    def by_inner(terms):
        terms = [[x.reshape(4, 4, n, width) for x in of_s] for of_s in terms]
        return [jnp.stack([total_of([x[:, i] for x in of_s]) for of_s in terms]) for i in range(4)]

    def inner_terms(terms):
        own, right, left, far = terms
        return scatter_direct([own] + [bf16(x) for x in (right, far, left)], False)

    partner = by_distance(swap(tokens, "xh"))
    plane1 = plane_of(by_distance(tokens))
    partner, plane1 = together(partner, plane1)
    plane0 = plane_of(partner)
    plane0, gate_q, up_q, down_q = together(plane0, gate_q, up_q, down_q)
    left, right = ring(plane0, True, 1), ring(plane0, True, -1)
    w0, w1 = scale_pair(gate_q, up_q, gate_scale, up_scale, groups)
    down_w = scale_one(down_q, down_scale)
    left, right, w0, w1, down_w = together(left, right, w0, w1, down_w)
    far_a, far_b = ring(left[:1], True, 1), ring(right[1:], True, -1)

    pieces0 = [plane0, right, left]
    sums0 = up_part(pieces0, w0)

    plane1, far_a, far_b, *sums0 = together(plane1, far_a, far_b, *sums0)
    pieces0.append([far_a, far_b])
    left, right = ring(plane1, True, 1), ring(plane1, True, -1)

    keep, send = up_part(pieces0[3:], w0, sums0)
    stay0, away0 = first_sum(keep, send)
    away0, pieces0[0] = together(away0, pieces0[0])
    got0 = swap(away0, "xl")
    keep, send = up_part(pieces0, w1)
    send, got0, left, right = together(send, got0, left, right)
    far_a, far_b = ring(left[:1], True, 1), ring(right[1:], True, -1)
    stay1, away1 = first_sum(keep, send)
    got1 = swap(away1, "xl")
    hid0 = activate(stay0, got0, groups[0])
    other0 = swap(hid0, "xl")

    pieces1 = [plane1, right, left]
    sums1 = up_part(pieces1, w0)
    got1, other0, *sums1 = together(got1, other0, *sums1)
    hid0 = (hid0, other0)

    hid1 = activate(stay1, got1, groups[1])
    hid1, far_a, far_b = together(hid1, far_a, far_b)
    pieces1.append([far_a, far_b])
    keep, send = up_part(pieces1[3:], w0, sums1)
    hid1, other1, send = together(hid1, swap(hid1, "xl"), send)
    hid = hidden_rows((hid0, (hid1, other1)))
    next_stay0, next_away0 = first_sum(keep, send)
    hid, next_away0 = together(hid, next_away0)
    next_got0 = swap(next_away0, "xl")

    far, early = down_first(hid)
    hid, pieces1[0], *far = together(hid, pieces1[0], *far)
    got = both_ways(far)
    early = both_ways(early)

    keep, send = up_part(pieces1, w1)
    send, next_got0, *got = together(send, next_got0, *got)
    stay1, away1 = first_sum(keep, send)
    hid0 = activate(next_stay0, next_got0, groups[0])
    hid0, away1, hid = together(hid0, away1, hid)
    got1 = swap(away1, "xl")
    other0 = swap(hid0, "xl")

    own, rest = down_rest(hid)
    got1, other0, *both = together(got1, other0, *join(got, rest), *early)
    late, early = both_ways(both[:2]), both[2:]

    hid1 = activate(stay1, got1, groups[1])
    hid = hidden_rows(((hid0, other0), (hid1, swap(hid1, "xl"))))
    sums0 = inner_terms(by_inner([[own[0], late[0], early[1]], [own[1], early[0], late[1]]]))
    far, early = down_first(hid)
    hid, *far = together(hid, *far)
    got = both_ways(far)
    early = both_ways(early)
    own, rest = down_rest(hid)
    rest[0], *both = together(rest[0], *got, *sums0[1:])
    got, sums0[1:] = both[:2], both[2:]
    crossing = swap(bf16(total_of(sums0)), "xh")
    late = both_ways(together(*join(got, rest)))
    crossing, *both = together(crossing, *late, *early)
    late, early = both[:2], both[2:]
    sums1 = inner_terms(by_inner([[own[0], late[0], early[1]], [own[1], early[0], late[1]]]))
    t = total_of(sums1) + f32(crossing)

    t = bf16(t).reshape(2, 2, 2, n, width).transpose(0, 2, 1, 3, 4)
    t = jnp.where(c == 1, t[:, :, ::-1], t)
    t = jnp.where(xl == 1, t[:, ::-1], t)
    return t.reshape(tokens.shape)


def solution(mesh):
    fine = Mesh(mesh.devices.reshape(SIZES), AXES)
    gx, gy = ("z", "y", "xh"), ("xl", "c")
    placed = (
        P(gx, gy),
        P(gy, gx),
        P(gy, gx),
        P(gy, gx),
        P(gy, gx),
        P(gx, gy),
        P(gx, gy),
    )
    return jax.shard_map(
        local, mesh=fine, in_specs=placed, out_specs=P(gx, gy), check_vma=False
    )
```

```python
import functools

import jax
import jax.numpy as jnp
from jax import lax
from jax.experimental import pallas as pl
from jax.experimental.pallas import tpu as pltpu
from jax.sharding import Mesh
from jax.sharding import PartitionSpec as P

AXES = ("z", "y", "xh", "xl", "c")
SIZES = (4, 4, 2, 2, 2)


def index_of(z, y, xh, xl, c):
    return (((z * 4 + y) * 2 + xh) * 2 + xl) * 2 + c


def every_device():
    for z in range(4):
        for y in range(4):
            for xh in range(2):
                for xl in range(2):
                    for c in range(2):
                        yield z, y, xh, xl, c


def ring_pairs(outer, step):
    pairs = []
    for z, y, xh, xl, c in every_device():
        if (c == 0) == outer:
            there = ((z + step) % 4, y, xh, xl, c)
        else:
            there = (z, (y + step) % 4, xh, xl, c)
        pairs.append((index_of(z, y, xh, xl, c), index_of(*there)))
    return pairs


def ring(x, outer, step):
    return lax.ppermute(x, AXES, ring_pairs(outer, step))


def swap(x, axis):
    return lax.ppermute(x, axis, [(0, 1), (1, 0)])


def scale_pair_kernel(gate_ref, up_ref, gate_s_ref, up_s_ref, *out_refs):
    for t in range(gate_ref.shape[0] // 128):
        rows = slice(t * 128, (t + 1) * 128)
        for at, (ref, s_ref) in enumerate(((gate_ref, gate_s_ref), (up_ref, up_s_ref))):
            value = (ref[rows, :].astype(jnp.float32) * s_ref[t : t + 1, :]).astype(jnp.bfloat16)
            first = 0
            for out_ref in out_refs:
                units = out_ref.shape[1] // 2
                out_ref[rows, at * units : (at + 1) * units] = value[:, first : first + units]
                first += units


def scale_pair(gate_q, up_q, gate_s, up_s, groups):
    rows, units = gate_q.shape
    block = 1024
    tiles = block // 128
    return pl.pallas_call(
        scale_pair_kernel,
        grid=(rows // block,),
        in_specs=[
            pl.BlockSpec((block, units), lambda i: (i, 0)),
            pl.BlockSpec((block, units), lambda i: (i, 0)),
            pl.BlockSpec((tiles, units), lambda i: (i, 0)),
            pl.BlockSpec((tiles, units), lambda i: (i, 0)),
        ],
        out_specs=[pl.BlockSpec((block, 2 * g), lambda i: (i, 0)) for g in groups],
        out_shape=[jax.ShapeDtypeStruct((rows, 2 * g), jnp.bfloat16) for g in groups],
        compiler_params=pltpu.CompilerParams(vmem_limit_bytes=40 * 1024 * 1024),
        cost_estimate=pl.CostEstimate(
            flops=2 * rows * units, bytes_accessed=8 * rows * units, transcendentals=0
        ),
    )(gate_q, up_q, jnp.repeat(gate_s, 128, axis=1), jnp.repeat(up_s, 128, axis=1))


def scale_one_kernel(q_ref, s_ref, out_ref):
    for t in range(q_ref.shape[0] // 128):
        rows = slice(t * 128, (t + 1) * 128)
        value = q_ref[rows, :].astype(jnp.float32) * s_ref[t : t + 1, :]
        out_ref[rows, :] = value.astype(jnp.bfloat16)


def scale_one(q, s):
    rows, cols = q.shape
    block = 1024
    return pl.pallas_call(
        scale_one_kernel,
        grid=(cols // block,),
        in_specs=[
            pl.BlockSpec((rows, block), lambda i: (0, i)),
            pl.BlockSpec((rows // 128, block), lambda i: (0, i)),
        ],
        out_specs=pl.BlockSpec((rows, block), lambda i: (0, i)),
        out_shape=jax.ShapeDtypeStruct((rows, cols), jnp.bfloat16),
        compiler_params=pltpu.CompilerParams(vmem_limit_bytes=40 * 1024 * 1024),
        cost_estimate=pl.CostEstimate(
            flops=rows * cols, bytes_accessed=4 * rows * cols, transcendentals=0
        ),
    )(q, jnp.repeat(s, 128, axis=1))


def f32(x):
    return x.astype(jnp.float32)


def bf16(x):
    return x.astype(jnp.bfloat16)


def together(*arrays):
    return lax.optimization_barrier(arrays)


def gather_direct(block, outer):
    return [block] + [ring(block, outer, step) for step in (-1, 2, 1)]


def scatter_direct(terms, outer):
    return [terms[0]] + [ring(terms[d], outer, step) for d, step in ((1, 1), (2, 2), (3, -1))]


def total_of(terms):
    return functools.reduce(jnp.add, (f32(t) for t in terms))


def up_kernel(parts, count, given, *refs):
    pieces, w_ref, x, sems = refs[:count], refs[count], refs[-2], refs[-1]
    outs = refs[count + 1 + given : -2]
    rows = pieces[0].shape[3]

    def copies(blocks, first):
        return [
            pltpu.make_async_copy(
                pieces[i].at[s, dc, dxl],
                x.at[pl.ds((first + k) * rows, rows), :],
                sems.at[first + k],
            )
            for k, (i, s, dc, dxl) in enumerate(blocks)
        ]

    def each():
        first = 0
        for out, at, blocks in parts:
            yield out, at * rows, blocks, first
            first += len(blocks)

    def put(out, at, value):
        outs[out][at : at + value.shape[0], :] = value.astype(jnp.bfloat16)

    def times(first, last):
        return jnp.dot(
            x[first * rows : last * rows, :], w_ref[...], preferred_element_type=jnp.float32
        )

    @pl.when(pl.program_id(0) == 0)
    def _():
        for _, _, blocks, first in each():
            for copy in copies(blocks, first):
                copy.start()
        for out, at, blocks, first in each():
            for copy in copies(blocks, first):
                copy.wait()
            put(out, at, times(first, first + len(blocks)))

    @pl.when(pl.program_id(0) != 0)
    def _():
        part = times(0, x.shape[0] // rows)
        for out, at, blocks, first in each():
            put(out, at, part[first * rows : (first + len(blocks)) * rows])


def up_part(pieces, w, into=None):
    arrays, places = [], []
    for piece in pieces:
        if isinstance(piece, list):
            places.append([(len(arrays) + s, 0) for s in range(2)])
            arrays.extend(piece)
        else:
            places.append([(len(arrays), s) for s in range(2)])
            arrays.append(piece)
    parts = []
    for dc in range(2):
        for at in range(0, len(places), 2):
            blocks = [
                (i, s, dc, dxl)
                for place in places[at : at + 2]
                for dxl in range(2)
                for i, s in place
            ]
            parts.append((dc, 4 * at, blocks))
    rows, width = arrays[0].shape[3:]
    columns = w.shape[1]
    block = 256
    count = 4 * len(pieces)
    given = [] if into is None else [o.reshape(16 * rows, columns) for o in into]
    place = 0 if into is None else 4 - len(pieces)
    outs = pl.pallas_call(
        functools.partial(up_kernel, parts, len(arrays), len(given)),
        grid=(columns // block,),
        in_specs=[pl.BlockSpec(memory_space=pl.ANY)] * len(arrays)
        + [pl.BlockSpec((width, block), lambda j: (0, j))]
        + [pl.BlockSpec(memory_space=pl.ANY)] * len(given),
        out_specs=[pl.BlockSpec((count * rows, block), lambda j: (place, j))] * 2,
        out_shape=[jax.ShapeDtypeStruct((16 * rows, columns), jnp.bfloat16)] * 2,
        scratch_shapes=[
            pltpu.VMEM((2 * count * rows, width), jnp.bfloat16),
            pltpu.SemaphoreType.DMA((2 * count,)),
        ],
        input_output_aliases={len(arrays) + 1 + i: i for i in range(len(given))},
        compiler_params=pltpu.CompilerParams(vmem_limit_bytes=20 * 1024 * 1024),
        cost_estimate=pl.CostEstimate(flops=1, bytes_accessed=1, transcendentals=0),
    )(*arrays, w, *given)
    return [o.reshape(4, 2, 2, rows, columns) for o in outs]


def down_kernel(x_ref, w_ref, *out_refs):
    out = jnp.dot(x_ref[...], w_ref[...], preferred_element_type=jnp.float32)
    first = 0
    for ref in out_refs:
        rows = ref.shape[0]
        ref[...] = out[first : first + rows].astype(jnp.bfloat16)
        first += rows


def down_part(x, w, sizes):
    rows, units = x.shape
    width = w.shape[1]
    block = 1024
    return pl.pallas_call(
        down_kernel,
        grid=(width // block,),
        in_specs=[
            pl.BlockSpec((rows, units), lambda j: (0, 0)),
            pl.BlockSpec((units, block), lambda j: (0, j)),
        ],
        out_specs=[pl.BlockSpec((size, block), lambda j: (0, j)) for size in sizes],
        out_shape=[jax.ShapeDtypeStruct((size, width), jnp.bfloat16) for size in sizes],
        compiler_params=pltpu.CompilerParams(vmem_limit_bytes=40 * 1024 * 1024),
        cost_estimate=pl.CostEstimate(flops=1, bytes_accessed=1, transcendentals=0),
    )(x, w)


def local(tokens, gate_q, gate_scale, up_q, up_scale, down_q, down_scale):
    width = tokens.shape[1]
    units = gate_q.shape[1]
    first = (units // 128 + 1) // 2 * 128
    groups = (first, units - first)
    n = tokens.shape[0] // 8
    slot = 2 * 4 * 4 * n
    half = slot // 2
    xl = lax.axis_index("xl")
    c = lax.axis_index("c")

    def by_distance(t):
        t = t.reshape(2, 2, 2, n, width)
        t = jnp.where(xl == 1, t[:, ::-1], t)
        t = jnp.where(c == 1, t[:, :, ::-1], t)
        return t.transpose(0, 2, 1, 3, 4)

    def plane_of(block):
        own, right, far, left = gather_direct(block, False)
        return jnp.stack([own, right, left, far], axis=3).reshape(2, 2, 2, 4 * n, width)

    def other_core(x):
        shape = x.shape
        x = swap(x, "c").reshape(4, -1, 4, n, shape[-1])
        return x.transpose(2, 1, 0, 3, 4).reshape(shape)

    def first_sum(keep, send):
        other = other_core(send)
        return (
            f32(keep[:, 0]) + f32(other[:, 0]),
            bf16(f32(keep[:, 1]) + f32(other[:, 1])),
        )

    def activate(stay, got, g):
        total = stay + f32(got)
        return bf16(jax.nn.silu(total[..., :g]) * total[..., g:])

    def hidden_rows(halves):
        near = jnp.concatenate([jnp.stack(h, axis=2) for h in halves], axis=-1)
        hid = jnp.stack([near, other_core(near)], axis=2)
        return hid.reshape(4, slot, units)

    def down_first(hid):
        _, right, left, far = hid
        x = jnp.concatenate([far, right[half:], left[:half]])
        outs = list(down_part(x, down_w, (half,) * 4))
        return outs[:2], outs[2:]

    def down_rest(hid):
        own, right, left, _ = hid
        x = jnp.concatenate([own, right[:half], left[half:]])
        outs = list(down_part(x, down_w, (half,) * 4))
        return outs[:2], outs[2:]

    def both_ways(terms):
        return [ring(terms[0], True, 1), ring(terms[1], True, -1)]

    def join(got, rest):
        return [bf16(f32(x) + f32(g)) for x, g in zip(rest, got)]

    def by_inner(terms):
        terms = [[x.reshape(4, 4, n, width) for x in of_s] for of_s in terms]
        return [jnp.stack([total_of([x[:, i] for x in of_s]) for of_s in terms]) for i in range(4)]

    def inner_terms(terms):
        own, right, left, far = terms
        return scatter_direct([own] + [bf16(x) for x in (right, far, left)], False)

    partner = by_distance(swap(tokens, "xh"))
    plane1 = plane_of(by_distance(tokens))
    partner, plane1 = together(partner, plane1)
    plane0 = plane_of(partner)
    plane0, gate_q, up_q, down_q = together(plane0, gate_q, up_q, down_q)
    left, right = ring(plane0, True, 1), ring(plane0, True, -1)
    w0, w1 = scale_pair(gate_q, up_q, gate_scale, up_scale, groups)
    down_w = scale_one(down_q, down_scale)
    left, right, w0, w1, down_w = together(left, right, w0, w1, down_w)
    far_a, far_b = ring(left[:1], True, 1), ring(right[1:], True, -1)

    pieces0 = [plane0, right, left]
    sums0 = up_part(pieces0, w0)

    plane1, far_a, far_b, *sums0 = together(plane1, far_a, far_b, *sums0)
    pieces0.append([far_a, far_b])
    left, right = ring(plane1, True, 1), ring(plane1, True, -1)

    keep, send = up_part(pieces0[3:], w0, sums0)
    stay0, away0 = first_sum(keep, send)
    away0, pieces0[0] = together(away0, pieces0[0])
    got0 = swap(away0, "xl")
    keep, send = up_part(pieces0, w1)
    send, got0, left, right = together(send, got0, left, right)
    far_a, far_b = ring(left[:1], True, 1), ring(right[1:], True, -1)
    stay1, away1 = first_sum(keep, send)
    got1 = swap(away1, "xl")
    hid0 = activate(stay0, got0, groups[0])
    other0 = swap(hid0, "xl")

    pieces1 = [plane1, right, left]
    sums1 = up_part(pieces1, w0)
    got1, other0, *sums1 = together(got1, other0, *sums1)
    hid0 = (hid0, other0)

    hid1 = activate(stay1, got1, groups[1])
    hid1, far_a, far_b = together(hid1, far_a, far_b)
    pieces1.append([far_a, far_b])
    keep, send = up_part(pieces1[3:], w0, sums1)
    hid1, other1, send = together(hid1, swap(hid1, "xl"), send)
    hid = hidden_rows((hid0, (hid1, other1)))
    next_stay0, next_away0 = first_sum(keep, send)
    hid, next_away0 = together(hid, next_away0)
    next_got0 = swap(next_away0, "xl")

    far, early = down_first(hid)
    hid, pieces1[0], *far = together(hid, pieces1[0], *far)
    got = both_ways(far)
    early = both_ways(early)

    keep, send = up_part(pieces1, w1)
    send, next_got0, *got = together(send, next_got0, *got)
    stay1, away1 = first_sum(keep, send)
    hid0 = activate(next_stay0, next_got0, groups[0])
    hid0, away1, hid = together(hid0, away1, hid)
    got1 = swap(away1, "xl")
    other0 = swap(hid0, "xl")

    own, rest = down_rest(hid)
    got1, other0, *both = together(got1, other0, *join(got, rest), *early)
    late, early = both_ways(both[:2]), both[2:]

    hid1 = activate(stay1, got1, groups[1])
    hid = hidden_rows(((hid0, other0), (hid1, swap(hid1, "xl"))))
    sums0 = inner_terms(by_inner([[own[0], late[0], early[1]], [own[1], early[0], late[1]]]))
    far, early = down_first(hid)
    hid, *far = together(hid, *far)
    got = both_ways(far)
    early = both_ways(early)
    own, rest = down_rest(hid)
    rest[0], *both = together(rest[0], *got, *sums0[1:])
    got, sums0[1:] = both[:2], both[2:]
    crossing = swap(bf16(total_of(sums0)), "xh")
    late = both_ways(together(*join(got, rest)))
    crossing, *both = together(crossing, *late, *early)
    late, early = both[:2], both[2:]
    sums1 = inner_terms(by_inner([[own[0], late[0], early[1]], [own[1], early[0], late[1]]]))
    t = total_of(sums1) + f32(crossing)

    t = bf16(t).reshape(2, 2, 2, n, width).transpose(0, 2, 1, 3, 4)
    t = jnp.where(c == 1, t[:, :, ::-1], t)
    t = jnp.where(xl == 1, t[:, ::-1], t)
    return t.reshape(tokens.shape)


def solution(mesh):
    fine = Mesh(mesh.devices.reshape(SIZES), AXES)
    gx, gy = ("z", "y", "xh"), ("xl", "c")
    placed = (
        P(gx, gy),
        P(gy, gx),
        P(gy, gx),
        P(gy, gx),
        P(gy, gx),
        P(gx, gy),
        P(gx, gy),
    )
    return jax.shard_map(
        local, mesh=fine, in_specs=placed, out_specs=P(gx, gy), check_vma=False
    )
```

```python
import functools

import jax
import jax.numpy as jnp
from jax import lax
from jax.experimental import pallas as pl
from jax.experimental.pallas import tpu as pltpu
from jax.sharding import Mesh
from jax.sharding import PartitionSpec as P

AXES = ("z", "y", "xh", "xl", "c")
SIZES = (4, 4, 2, 2, 2)


def index_of(z, y, xh, xl, c):
    return (((z * 4 + y) * 2 + xh) * 2 + xl) * 2 + c


def every_device():
    for z in range(4):
        for y in range(4):
            for xh in range(2):
                for xl in range(2):
                    for c in range(2):
                        yield z, y, xh, xl, c


def ring_pairs(outer, step):
    pairs = []
    for z, y, xh, xl, c in every_device():
        if (c == 0) == outer:
            there = ((z + step) % 4, y, xh, xl, c)
        else:
            there = (z, (y + step) % 4, xh, xl, c)
        pairs.append((index_of(z, y, xh, xl, c), index_of(*there)))
    return pairs


def ring(x, outer, step):
    return lax.ppermute(x, AXES, ring_pairs(outer, step))


def swap(x, axis):
    return lax.ppermute(x, axis, [(0, 1), (1, 0)])


def scale_pair_kernel(gate_ref, up_ref, gate_s_ref, up_s_ref, *out_refs):
    for t in range(gate_ref.shape[0] // 128):
        rows = slice(t * 128, (t + 1) * 128)
        for at, (ref, s_ref) in enumerate(((gate_ref, gate_s_ref), (up_ref, up_s_ref))):
            value = (ref[rows, :].astype(jnp.float32) * s_ref[t : t + 1, :]).astype(jnp.bfloat16)
            first = 0
            for out_ref in out_refs:
                units = out_ref.shape[1] // 2
                out_ref[rows, at * units : (at + 1) * units] = value[:, first : first + units]
                first += units


def scale_pair(gate_q, up_q, gate_s, up_s, groups):
    rows, units = gate_q.shape
    block = 1024
    tiles = block // 128
    return pl.pallas_call(
        scale_pair_kernel,
        grid=(rows // block,),
        in_specs=[
            pl.BlockSpec((block, units), lambda i: (i, 0)),
            pl.BlockSpec((block, units), lambda i: (i, 0)),
            pl.BlockSpec((tiles, units), lambda i: (i, 0)),
            pl.BlockSpec((tiles, units), lambda i: (i, 0)),
        ],
        out_specs=[pl.BlockSpec((block, 2 * g), lambda i: (i, 0)) for g in groups],
        out_shape=[jax.ShapeDtypeStruct((rows, 2 * g), jnp.bfloat16) for g in groups],
        compiler_params=pltpu.CompilerParams(vmem_limit_bytes=40 * 1024 * 1024),
        cost_estimate=pl.CostEstimate(
            flops=2 * rows * units, bytes_accessed=8 * rows * units, transcendentals=0
        ),
    )(gate_q, up_q, jnp.repeat(gate_s, 128, axis=1), jnp.repeat(up_s, 128, axis=1))


def scale_one_kernel(q_ref, s_ref, out_ref):
    for t in range(q_ref.shape[0] // 128):
        rows = slice(t * 128, (t + 1) * 128)
        value = q_ref[rows, :].astype(jnp.float32) * s_ref[t : t + 1, :]
        out_ref[rows, :] = value.astype(jnp.bfloat16)


def scale_one(q, s):
    rows, cols = q.shape
    block = 1024
    return pl.pallas_call(
        scale_one_kernel,
        grid=(cols // block,),
        in_specs=[
            pl.BlockSpec((rows, block), lambda i: (0, i)),
            pl.BlockSpec((rows // 128, block), lambda i: (0, i)),
        ],
        out_specs=pl.BlockSpec((rows, block), lambda i: (0, i)),
        out_shape=jax.ShapeDtypeStruct((rows, cols), jnp.bfloat16),
        compiler_params=pltpu.CompilerParams(vmem_limit_bytes=40 * 1024 * 1024),
        cost_estimate=pl.CostEstimate(
            flops=rows * cols, bytes_accessed=4 * rows * cols, transcendentals=0
        ),
    )(q, jnp.repeat(s, 128, axis=1))


def f32(x):
    return x.astype(jnp.float32)


def bf16(x):
    return x.astype(jnp.bfloat16)


def together(*arrays):
    return lax.optimization_barrier(arrays)


def gather_direct(block, outer):
    return [block] + [ring(block, outer, step) for step in (-1, 2, 1)]


def scatter_direct(terms, outer):
    return [terms[0]] + [ring(terms[d], outer, step) for d, step in ((1, 1), (2, 2), (3, -1))]


def total_of(terms):
    return functools.reduce(jnp.add, (f32(t) for t in terms))


def up_kernel(parts, count, given, *refs):
    pieces, w_ref, x, sems = refs[:count], refs[count], refs[-2], refs[-1]
    outs = refs[count + 1 + given : -2]
    rows = pieces[0].shape[3]

    def copies(blocks, first):
        return [
            pltpu.make_async_copy(
                pieces[i].at[s, dc, dxl],
                x.at[pl.ds((first + k) * rows, rows), :],
                sems.at[first + k],
            )
            for k, (i, s, dc, dxl) in enumerate(blocks)
        ]

    def each():
        first = 0
        for out, at, blocks in parts:
            yield out, at * rows, blocks, first
            first += len(blocks)

    def put(out, at, value):
        outs[out][at : at + value.shape[0], :] = value.astype(jnp.bfloat16)

    def times(first, last):
        return jnp.dot(
            x[first * rows : last * rows, :], w_ref[...], preferred_element_type=jnp.float32
        )

    @pl.when(pl.program_id(0) == 0)
    def _():
        for _, _, blocks, first in each():
            for copy in copies(blocks, first):
                copy.start()
        for out, at, blocks, first in each():
            for copy in copies(blocks, first):
                copy.wait()
            put(out, at, times(first, first + len(blocks)))

    @pl.when(pl.program_id(0) != 0)
    def _():
        part = times(0, x.shape[0] // rows)
        for out, at, blocks, first in each():
            put(out, at, part[first * rows : (first + len(blocks)) * rows])


def up_part(pieces, w, into=None):
    arrays, places = [], []
    for piece in pieces:
        if isinstance(piece, list):
            places.append([(len(arrays) + s, 0) for s in range(2)])
            arrays.extend(piece)
        else:
            places.append([(len(arrays), s) for s in range(2)])
            arrays.append(piece)
    parts = []
    for dc in range(2):
        for at in range(0, len(places), 2):
            blocks = [
                (i, s, dc, dxl)
                for place in places[at : at + 2]
                for dxl in range(2)
                for i, s in place
            ]
            parts.append((dc, 4 * at, blocks))
    rows, width = arrays[0].shape[3:]
    columns = w.shape[1]
    block = 256
    count = 4 * len(pieces)
    given = [] if into is None else [o.reshape(16 * rows, columns) for o in into]
    place = 0 if into is None else 4 - len(pieces)
    outs = pl.pallas_call(
        functools.partial(up_kernel, parts, len(arrays), len(given)),
        grid=(columns // block,),
        in_specs=[pl.BlockSpec(memory_space=pl.ANY)] * len(arrays)
        + [pl.BlockSpec((width, block), lambda j: (0, j))]
        + [pl.BlockSpec(memory_space=pl.ANY)] * len(given),
        out_specs=[pl.BlockSpec((count * rows, block), lambda j: (place, j))] * 2,
        out_shape=[jax.ShapeDtypeStruct((16 * rows, columns), jnp.bfloat16)] * 2,
        scratch_shapes=[
            pltpu.VMEM((2 * count * rows, width), jnp.bfloat16),
            pltpu.SemaphoreType.DMA((2 * count,)),
        ],
        input_output_aliases={len(arrays) + 1 + i: i for i in range(len(given))},
        compiler_params=pltpu.CompilerParams(vmem_limit_bytes=20 * 1024 * 1024),
        cost_estimate=pl.CostEstimate(flops=1, bytes_accessed=1, transcendentals=0),
    )(*arrays, w, *given)
    return [o.reshape(4, 2, 2, rows, columns) for o in outs]


def down_kernel(x_ref, w_ref, *out_refs):
    out = jnp.dot(x_ref[...], w_ref[...], preferred_element_type=jnp.float32)
    first = 0
    for ref in out_refs:
        rows = ref.shape[0]
        ref[...] = out[first : first + rows].astype(jnp.bfloat16)
        first += rows


def down_part(x, w, sizes):
    rows, units = x.shape
    width = w.shape[1]
    block = 1024
    return pl.pallas_call(
        down_kernel,
        grid=(width // block,),
        in_specs=[
            pl.BlockSpec((rows, units), lambda j: (0, 0)),
            pl.BlockSpec((units, block), lambda j: (0, j)),
        ],
        out_specs=[pl.BlockSpec((size, block), lambda j: (0, j)) for size in sizes],
        out_shape=[jax.ShapeDtypeStruct((size, width), jnp.bfloat16) for size in sizes],
        compiler_params=pltpu.CompilerParams(vmem_limit_bytes=40 * 1024 * 1024),
        cost_estimate=pl.CostEstimate(flops=1, bytes_accessed=1, transcendentals=0),
    )(x, w)


def local(tokens, gate_q, gate_scale, up_q, up_scale, down_q, down_scale):
    width = tokens.shape[1]
    units = gate_q.shape[1]
    first = (units // 128 + 1) // 2 * 128
    groups = (first, units - first)
    n = tokens.shape[0] // 8
    slot = 2 * 4 * 4 * n
    half = slot // 2
    xl = lax.axis_index("xl")
    c = lax.axis_index("c")

    def by_distance(t):
        t = t.reshape(2, 2, 2, n, width)
        t = jnp.where(xl == 1, t[:, ::-1], t)
        t = jnp.where(c == 1, t[:, :, ::-1], t)
        return t.transpose(0, 2, 1, 3, 4)

    def plane_of(block):
        own, right, far, left = gather_direct(block, False)
        return jnp.stack([own, right, left, far], axis=3).reshape(2, 2, 2, 4 * n, width)

    def other_core(x):
        shape = x.shape
        x = swap(x, "c").reshape(4, -1, 4, n, shape[-1])
        return x.transpose(2, 1, 0, 3, 4).reshape(shape)

    def first_sum(keep, send):
        other = other_core(send)
        return (
            f32(keep[:, 0]) + f32(other[:, 0]),
            bf16(f32(keep[:, 1]) + f32(other[:, 1])),
        )

    def activate(stay, got, g):
        total = stay + f32(got)
        return bf16(jax.nn.silu(total[..., :g]) * total[..., g:])

    def hidden_rows(halves):
        near = jnp.concatenate([jnp.stack(h, axis=2) for h in halves], axis=-1)
        hid = jnp.stack([near, other_core(near)], axis=2)
        return hid.reshape(4, slot, units)

    def down_first(hid):
        _, right, left, far = hid
        x = jnp.concatenate([far, right[half:], left[:half]])
        outs = list(down_part(x, down_w, (half,) * 4))
        return outs[:2], outs[2:]

    def down_rest(hid):
        own, right, left, _ = hid
        x = jnp.concatenate([own, right[:half], left[half:]])
        outs = list(down_part(x, down_w, (half,) * 4))
        return outs[:2], outs[2:]

    def both_ways(terms):
        return [ring(terms[0], True, 1), ring(terms[1], True, -1)]

    def join(got, rest):
        return [bf16(f32(x) + f32(g)) for x, g in zip(rest, got)]

    def by_inner(terms):
        terms = [[x.reshape(4, 4, n, width) for x in of_s] for of_s in terms]
        return [jnp.stack([total_of([x[:, i] for x in of_s]) for of_s in terms]) for i in range(4)]

    def inner_terms(terms):
        own, right, left, far = terms
        return scatter_direct([own] + [bf16(x) for x in (right, far, left)], False)

    partner = by_distance(swap(tokens, "xh"))
    plane1 = plane_of(by_distance(tokens))
    partner, plane1 = together(partner, plane1)
    own, right, far, left = gather_direct(partner, False)
    plane0 = [
        jnp.stack([x[s : s + 1] for x in (own, right, left, far)], axis=3).reshape(
            1, 2, 2, 4 * n, width
        )
        for s in range(2)
    ]
    plane0, gate_q, up_q, down_q = together(plane0, gate_q, up_q, down_q)
    left = [ring(x, True, 1) for x in plane0]
    right = [ring(x, True, -1) for x in plane0]
    w0, w1 = scale_pair(gate_q, up_q, gate_scale, up_scale, groups)
    down_w = scale_one(down_q, down_scale)
    left, right, w0, w1, down_w = together(left, right, w0, w1, down_w)
    far_a, far_b = ring(left[0], True, 1), ring(right[1], True, -1)

    pieces0 = [plane0, right, left]
    sums0 = up_part(pieces0, w0)

    plane1, far_a, far_b, *sums0 = together(plane1, far_a, far_b, *sums0)
    pieces0.append([far_a, far_b])
    left, right = ring(plane1, True, 1), ring(plane1, True, -1)

    keep, send = up_part(pieces0[3:], w0, sums0)
    stay0, away0 = first_sum(keep, send)
    away0, pieces0[0] = together(away0, pieces0[0])
    got0 = swap(away0, "xl")
    keep, send = up_part(pieces0, w1)
    send, got0, left, right = together(send, got0, left, right)
    far_a, far_b = ring(left[:1], True, 1), ring(right[1:], True, -1)
    stay1, away1 = first_sum(keep, send)
    got1 = swap(away1, "xl")
    hid0 = activate(stay0, got0, groups[0])
    other0 = swap(hid0, "xl")

    pieces1 = [plane1, right, left]
    sums1 = up_part(pieces1, w0)
    got1, other0, *sums1 = together(got1, other0, *sums1)
    hid0 = (hid0, other0)

    hid1 = activate(stay1, got1, groups[1])
    hid1, far_a, far_b = together(hid1, far_a, far_b)
    pieces1.append([far_a, far_b])
    keep, send = up_part(pieces1[3:], w0, sums1)
    hid1, other1, send = together(hid1, swap(hid1, "xl"), send)
    hid = hidden_rows((hid0, (hid1, other1)))
    next_stay0, next_away0 = first_sum(keep, send)
    hid, next_away0 = together(hid, next_away0)
    next_got0 = swap(next_away0, "xl")

    far, early = down_first(hid)
    hid, pieces1[0], *far = together(hid, pieces1[0], *far)
    got = both_ways(far)
    early = both_ways(early)

    keep, send = up_part(pieces1, w1)
    send, next_got0, *got = together(send, next_got0, *got)
    stay1, away1 = first_sum(keep, send)
    hid0 = activate(next_stay0, next_got0, groups[0])
    hid0, away1, hid = together(hid0, away1, hid)
    got1 = swap(away1, "xl")
    other0 = swap(hid0, "xl")

    own, rest = down_rest(hid)
    got1, other0, *both = together(got1, other0, *join(got, rest), *early)
    late, early = both_ways(both[:2]), both[2:]

    hid1 = activate(stay1, got1, groups[1])
    hid = hidden_rows(((hid0, other0), (hid1, swap(hid1, "xl"))))
    sums0 = inner_terms(by_inner([[own[0], late[0], early[1]], [own[1], early[0], late[1]]]))
    far, early = down_first(hid)
    hid, *far = together(hid, *far)
    got = both_ways(far)
    early = both_ways(early)
    own, rest = down_rest(hid)
    rest[0], *both = together(rest[0], *got, *sums0[1:])
    got, sums0[1:] = both[:2], both[2:]
    crossing = swap(bf16(total_of(sums0)), "xh")
    late = both_ways(together(*join(got, rest)))
    crossing, *both = together(crossing, *late, *early)
    late, early = both[:2], both[2:]
    sums1 = inner_terms(by_inner([[own[0], late[0], early[1]], [own[1], early[0], late[1]]]))
    t = total_of(sums1) + f32(crossing)

    t = bf16(t).reshape(2, 2, 2, n, width).transpose(0, 2, 1, 3, 4)
    t = jnp.where(c == 1, t[:, :, ::-1], t)
    t = jnp.where(xl == 1, t[:, ::-1], t)
    return t.reshape(tokens.shape)


def solution(mesh):
    fine = Mesh(mesh.devices.reshape(SIZES), AXES)
    gx, gy = ("z", "y", "xh"), ("xl", "c")
    placed = (
        P(gx, gy),
        P(gy, gx),
        P(gy, gx),
        P(gy, gx),
        P(gy, gx),
        P(gx, gy),
        P(gx, gy),
    )
    return jax.shard_map(
        local, mesh=fine, in_specs=placed, out_specs=P(gx, gy), check_vma=False
    )
```
